32 devices in a mesh: ctx: 4 (over z), tp: 8 (over y, x, core).
Axes of the slice: x: 2, y: 2, z: 4, core: 2. Of those that a mesh axis runs over, the one named last changes fastest.
Arguments:
- queries: bfloat16 [2048, 4096], P('ctx', 'tp'), may hold values from -15 to 15
- keys: bfloat16 [2048, 1024], P('ctx', 'tp'), may hold values from -15 to 15, as said below
- values: bfloat16 [2048, 1024], P('ctx', 'tp'), may hold values from -6 to 6, as said below
- doc_blocks: int32 [16], replicated, may hold values from 0 to 5, never falling along the last dimension, each value on 1 to 8 neighbouring positions
Outputs:
- attended: bfloat16 [2048, 4096], P('ctx', 'tp')
The draws below stay inside these ranges and needn't reach their ends.
Inputs may be any that keep to these rules, and one draw needn't show every extreme that they name: `doc_blocks`: ids never fall along the row; each document covers 1 to 8 blocks and one covers exactly that many. `keys`: copies of the same key-value head are equal. `values`: copies of the same key-value head are equal.
All inputs are finite; a program needn't handle non-finite values.
Results may differ from the reference program's by a relative error of at most 0.0047.
Values may be sent and summed in bfloat16 or wider, within the bound.
No kernel may reach another device: no remote copies, remote signals or barrier semaphores. Data moves between devices by JAX's collectives and lax.ppermute only.
A program may use at most 64 MiB of HBM per device.

```python
import math
import jax
import jax.numpy as jnp
import numpy as np
from jax import lax

HQ = 32
KVH = 8
HD = 128
BLK = 128
COUNT = 6
CH = 256
L = 2048
S = 16
COPIES = 8
N_CTX = 4


def replicate_heads(array):
    spread = COPIES // KVH
    grouped = array.reshape(L, KVH, 1, HD)
    return jnp.broadcast_to(grouped, (L, KVH, spread, HD)).reshape(L, COPIES * HD)


def drawn_pair(key):
    base = jax.random.fold_in(key, 11)
    first_key, second_key = jax.random.split(base, 2)
    query_part = jnp.clip(jax.random.normal(first_key, (L, HQ * HD), jnp.float32), -4.0, 4.0)
    key_part = jnp.clip(jax.random.normal(second_key, (L, KVH * HD), jnp.float32), -4.0, 4.0)
    return (query_part, key_part)


def draw_queries(key, part):
    return drawn_pair(key)[0].astype(jnp.bfloat16)


def draw_keys(key, part):
    return replicate_heads(drawn_pair(key)[1]).astype(jnp.bfloat16)


def draw_values(key, part):
    value_key = jax.random.fold_in(key, 23)
    drawn = jnp.clip(jax.random.normal(value_key, (L, KVH * HD), jnp.float32), -6.0, 6.0)
    return replicate_heads(drawn).astype(jnp.bfloat16)


def split_up(number_of, total, limit, slope):
    portions = [(1 << 20) // math.isqrt(grade ** slope) + 1 for grade in range(2, number_of + 1)]
    surplus, counts = total - limit - (number_of - 1), [1] * (number_of - 1)
    while surplus > 0:
        candidates = [i for i in range(number_of - 1) if counts[i] < limit]
        whole, budget = sum([portions[i] for i in candidates]), surplus
        for i in candidates:
            more = min(limit - counts[i], max(1, budget * portions[i] // whole), surplus)
            counts[i] = counts[i] + more
            surplus = surplus - more
    return np.array([limit] + counts)


def uneven_parts(rng, amount, total, reach, skew):
    if amount == 2:
        one = jax.random.randint(rng, (), max(1, total - reach), min(reach, total - 1) + 1)
        return jnp.stack([one, total - one])
    tallies = jnp.asarray(split_up(amount, total, reach, skew), jnp.int32)
    couples = (amount - 1) // 2
    source_of, receiver = tallies[1:1 + 2 * couples:2], tallies[2:2 + 2 * couples:2]
    margin = jnp.minimum(source_of - 1, reach - receiver)
    moved = jax.random.randint(jax.random.fold_in(rng, 1), (couples,), 0, 1 << 20) % (margin + 1)
    tallies = tallies.at[1:1 + 2 * couples:2].set(source_of - moved).at[2:2 + 2 * couples:2].set(receiver + moved)
    return tallies[jax.random.permutation(jax.random.fold_in(rng, 2), amount)]


def setup_inputs(seed: int = 0) -> dict:
    streams_of = jax.random.split(jax.random.key(seed), 5)
    return {
        "queries": draw_queries(jax.random.fold_in(streams_of[4], 71), 0),
        "keys": draw_keys(jax.random.fold_in(streams_of[4], 71), 0),
        "values": draw_values(jax.random.fold_in(streams_of[4], 71), 0),
        "doc_blocks": jnp.searchsorted(jnp.cumsum(uneven_parts(streams_of[3], COUNT, S, S // 2, 0)), jnp.arange(S), side="right").astype(jnp.int32),
    }


def reference(queries, keys, values, doc_blocks):
    total_spans = 2 * N_CTX
    order_table = np.array([j // 2 if j % 2 == 0 else total_spans - 1 - j // 2 for j in range(total_spans)])
    inverse_table = np.argsort(order_table)

    def to_row_order(array):
        return array.reshape(total_spans, CH, array.shape[1])[inverse_table].reshape(L, array.shape[1])

    repeat_count = HQ // COPIES
    query_rows = to_row_order(queries).reshape(L, COPIES, repeat_count, HD)
    key_rows = to_row_order(keys).astype(jnp.float32).reshape(L, COPIES, HD).transpose(1, 0, 2)
    value_rows = to_row_order(values).astype(jnp.float32).reshape(L, COPIES, HD).transpose(1, 0, 2)
    doc_rows = jnp.repeat(doc_blocks, BLK).astype(jnp.int32)
    key_pos = jnp.arange(L, dtype=jnp.int32)
    score_scale = HD ** -0.5

    def one_span(index):
        start = (index * CH).astype(jnp.int32)
        query_part = lax.dynamic_slice_in_dim(query_rows, start, CH, 0).astype(jnp.float32).transpose(1, 0, 2, 3)
        query_doc = lax.dynamic_slice_in_dim(doc_rows, start, CH, 0)
        query_pos = start + jnp.arange(CH, dtype=jnp.int32)
        allowed = (query_doc[:, None] == doc_rows[None, :]) & (key_pos[None, :] <= query_pos[:, None])

        def one_copy(item):
            query_copy, key_copy, value_copy = item
            scores = jnp.einsum("qrd,kd->rqk", query_copy, key_copy) * score_scale
            scores = jnp.where(allowed, scores, -1e30)
            peak_value = jnp.max(scores, axis=-1, keepdims=True)
            weight = jnp.where(allowed, jnp.exp(scores - peak_value), 0.0)
            total = jnp.sum(weight, axis=-1, keepdims=True)
            probs = (weight / total).astype(jnp.bfloat16)
            probs = lax.optimization_barrier(probs).astype(jnp.float32)
            return jnp.einsum("rqk,kd->qrd", probs, value_copy)

        mixed = lax.map(one_copy, (query_part, key_rows, value_rows))
        return mixed.transpose(1, 0, 2, 3).reshape(CH, HQ * HD).astype(jnp.bfloat16)

    outputs = lax.map(one_span, jnp.arange(total_spans, dtype=jnp.int32))
    return outputs[order_table].reshape(L, HQ * HD)
```

```python
import math

import jax
import jax.numpy as jnp
from jax import lax
from jax.experimental import pallas as pl
from jax.experimental.pallas import tpu as pltpu
from jax.sharding import PartitionSpec as P

HD = 128
BLK = 128
MASKED = -1e30
SCALE2 = HD ** (-0.5) * math.log2(math.e)
VMEM = pl.BlockSpec(memory_space=pltpu.VMEM)
SMEM = pl.BlockSpec(memory_space=pltpu.SMEM)


def pack_kernel(shards, k_ref, v_ref, doc_ref, both_ref, *refs):
    sends, plan_ref = refs[:-1], refs[-1]
    me = lax.axis_index("ctx")
    span = k_ref.shape[0] // 2
    per_span = span // BLK
    for r, send in enumerate(sends, 1):
        row = pl.multiple_of(jnp.where((me ^ r) > me, 0, span), span)
        send[:span, :] = k_ref[pl.ds(row, span), :]
        send[span:, :] = v_ref[pl.ds(row, span), :]
    both_ref[: 2 * span, :] = k_ref[...]
    both_ref[2 * span :, :] = v_ref[...]
    wide = jnp.int32(0)
    for s in range(1, shards):
        last = doc_ref[per_span * (s + 1) - 1]
        first = doc_ref[per_span * (2 * shards - s)]
        wide = jnp.where(last == first, 1, wide)
    plan_ref[0] = wide


def attend_kernel(shards, sources, q_ref, k_ref, v_ref, doc_ref, *refs):
    received, (o_ref, m_ref, acc_ref) = refs[:-3], refs[-3:]
    me = lax.axis_index("ctx")
    span = k_ref.shape[0] // 2
    per_span = span // BLK
    chunk = min(span, 2 * BLK)
    blocks = chunk // BLK
    chunks = span // chunk
    heads = q_ref.shape[1] // HD
    spans = (me, 2 * shards - 1 - me)
    row_in = lax.broadcasted_iota(jnp.int32, (BLK, BLK), 0)
    col_in = lax.broadcasted_iota(jnp.int32, (BLK, BLK), 1)
    triangle = jnp.where(col_in <= row_in, 0.0, MASKED).astype(jnp.float32)
    ones = jnp.ones((chunk, HD), jnp.bfloat16)

    def tile(t, query_chunk, key_chunk, source, key_span, diagonal, first):
        keys, key_row, values, value_row = source
        query_row = t * span + query_chunk * chunk
        key_rows = pl.ds(pl.multiple_of(key_row + key_chunk * chunk, BLK), chunk)
        value_rows = pl.ds(pl.multiple_of(value_row + key_chunk * chunk, BLK), chunk)
        rows = pl.ds(pl.multiple_of(query_row, BLK), chunk)
        query_block = spans[t] * per_span + query_chunk * blocks
        key_block = key_span * per_span + key_chunk * blocks
        bias = {}
        for a in range(blocks):
            for c in range(blocks):
                same = doc_ref[query_block + a] == doc_ref[key_block + c]
                if diagonal and c > a:
                    same = jnp.bool_(False)
                bias[a, c] = jnp.where(same, 0.0, MASKED).astype(jnp.float32)
        key = keys[key_rows, :]
        value = jnp.concatenate([values[value_rows, :], ones], axis=1)
        for h in range(heads):
            query = q_ref[rows, h * HD : (h + 1) * HD]
            scores = lax.dot_general(
                query, key, (((1,), (1,)), ((), ())), preferred_element_type=jnp.float32
            )
            parts = []
            for a in range(blocks):
                line = []
                for c in range(blocks):
                    part = scores[a * BLK : (a + 1) * BLK, c * BLK : (c + 1) * BLK]
                    part = part + bias[a, c]
                    if diagonal and a == c:
                        part = part + triangle
                    line.append(part)
                parts.append(line)
            peak = jnp.concatenate(
                [
                    jnp.broadcast_to(
                        jnp.max(
                            line[0] if blocks == 1 else jnp.maximum(*line),
                            axis=1,
                            keepdims=True,
                        ),
                        (BLK, HD),
                    )
                    for line in parts
                ],
                axis=0,
            )
            if not first:
                before = m_ref[h, rows, :]
                peak = jnp.maximum(peak, before)
            weights = jnp.concatenate(
                [
                    jnp.concatenate(
                        [
                            jnp.exp2((part - peak[a * BLK : (a + 1) * BLK]) * SCALE2)
                            for part in line
                        ],
                        axis=1,
                    )
                    for a, line in enumerate(parts)
                ],
                axis=0,
            ).astype(jnp.bfloat16)
            mixed = jnp.dot(weights, value, preferred_element_type=jnp.float32)
            if not first:
                shrink = jnp.exp2((before - peak) * SCALE2)
                mixed = mixed + acc_ref[h, rows, :] * jnp.concatenate([shrink, shrink], axis=1)
            m_ref[h, rows, :] = peak
            acc_ref[h, rows, :] = mixed

    def needed(t, query_chunk, key_chunk, key_span):
        last = doc_ref[key_span * per_span + (key_chunk + 1) * blocks - 1]
        first = doc_ref[spans[t] * per_span + query_chunk * blocks]
        return last == first

    def whole_span(t, source, key_span, earlier):
        def step(index, carry):
            query_chunk, key_chunk = index // chunks, index % chunks

            @pl.when(earlier & needed(t, query_chunk, key_chunk, key_span))
            def _():
                tile(t, query_chunk, key_chunk, source, key_span, False, False)

            return carry

        lax.fori_loop(0, chunks * chunks, step, 0)

    own = [(k_ref, 0, v_ref, 0), (k_ref, span, v_ref, span)]
    for t in range(2):

        def diagonal_step(index, carry):
            tile(t, index, index, own[t], spans[t], True, True)

            def before_step(key_chunk, inner):
                @pl.when(needed(t, index, key_chunk, spans[t]))
                def _():
                    tile(t, index, key_chunk, own[t], spans[t], False, False)

                return inner

            if chunks > 1:
                lax.fori_loop(0, index, before_step, 0)
            return carry

        lax.fori_loop(0, chunks, diagonal_step, 0)
    if sources == "gathered":
        all_keys, all_values = received
        for t in range(2):

            def span_step(s, carry, t=t):
                holder = jnp.minimum(s, 2 * shards - 1 - s)
                row = (2 * holder + jnp.where(s < shards, 0, 1)) * span
                whole_span(t, (all_keys, row, all_values, row), s, jnp.bool_(True))
                return carry

            lax.fori_loop(0, spans[t], span_step, 0)
        sources = []
    else:
        whole_span(1, own[0], spans[0], jnp.bool_(True))
    for r, kind in sources:
        ref = received[r - 1]
        partner = me ^ r
        if kind == "one":
            key_span = jnp.where(partner < me, partner, 2 * shards - 1 - partner)
            found = [((ref, 0, ref, span), key_span)]
        else:
            found = [
                ((ref, 0, ref, 2 * span), partner),
                ((ref, span, ref, 3 * span), 2 * shards - 1 - partner),
            ]
        for source, key_span in found:
            for t in range(2):
                whole_span(t, source, key_span, key_span < spans[t])

    for h in range(heads):
        total = acc_ref[h, :, HD:]
        o_ref[:, h * HD : (h + 1) * HD] = (acc_ref[h, :, :HD] / total).astype(jnp.bfloat16)


def body(queries, keys, values, doc_blocks):
    shards = lax.axis_size("ctx")
    rows, heads = queries.shape[0], queries.shape[1] // HD
    span = rows // 2
    send_shape = jax.ShapeDtypeStruct((2 * span, HD), jnp.bfloat16)
    both_shape = jax.ShapeDtypeStruct((4 * span, HD), jnp.bfloat16)
    partners = range(1, shards)

    def attend(sources, received):
        return pl.pallas_call(
            lambda *refs: attend_kernel(shards, sources, *refs),
            in_specs=[VMEM, VMEM, VMEM, SMEM] + [VMEM] * len(received),
            out_specs=VMEM,
            out_shape=jax.ShapeDtypeStruct(queries.shape, jnp.bfloat16),
            scratch_shapes=[
                pltpu.VMEM((heads, rows, HD), jnp.float32),
                pltpu.VMEM((heads, rows, 2 * HD), jnp.float32),
            ],
            compiler_params=pltpu.CompilerParams(vmem_limit_bytes=48 * 1024 * 1024),
            name="attend",
        )(queries, keys, values, doc_blocks, *received)

    if shards != 4:
        received = [lax.all_gather(x, "ctx", axis=0, tiled=True) for x in (keys, values)]
        return attend("gathered", received)

    both, *sends, plan = pl.pallas_call(
        lambda *refs: pack_kernel(shards, *refs),
        in_specs=[VMEM, VMEM, SMEM],
        out_specs=[VMEM] * shards + [SMEM],
        out_shape=[both_shape]
        + [send_shape] * (shards - 1)
        + [jax.ShapeDtypeStruct((1,), jnp.int32)],
        name="pack",
    )(keys, values, doc_blocks)

    def swap(array, r):
        return lax.ppermute(array, "ctx", [(i, i ^ r) for i in range(shards)])

    def narrow(_):
        received = [swap(sends[r - 1], r) for r in partners]
        return attend([(r, "one") for r in partners], received)

    def wide(_):
        received = [swap(both, r) for r in partners]
        return attend([(r, "two") for r in partners], received)

    return lax.switch(plan[0], [narrow, wide], 0)


def solution(mesh):
    return jax.shard_map(
        body,
        mesh=mesh,
        in_specs=(P("ctx", "tp"), P("ctx", "tp"), P("ctx", "tp"), P()),
        out_specs=P("ctx", "tp"),
        check_vma=False,
    )
```

```python
import math

import jax
import jax.numpy as jnp
from jax import lax
from jax.experimental import pallas as pl
from jax.experimental.pallas import tpu as pltpu
from jax.sharding import PartitionSpec as P

HD = 128
BLK = 128
MASKED = -1e30
SCALE2 = HD ** (-0.5) * math.log2(math.e)
VMEM = pl.BlockSpec(memory_space=pltpu.VMEM)
SMEM = pl.BlockSpec(memory_space=pltpu.SMEM)


ANY = pl.BlockSpec(memory_space=pl.ANY)


def normalised(mixed):
    inverse = pl.reciprocal(mixed[:, HD:], approx=True)
    inverse = inverse * (2.0 - mixed[:, HD:] * inverse)
    return (mixed[:, :HD] * inverse).astype(jnp.bfloat16)


class Tiles:
    def __init__(self, shards, span, heads, q_ref, doc_ref, m_ref, acc_ref):
        self.span, self.heads = span, heads
        self.q_ref, self.doc_ref, self.m_ref, self.acc_ref = q_ref, doc_ref, m_ref, acc_ref
        self.me = lax.axis_index("ctx")
        self.per_span = span // BLK
        self.chunk = min(span, 2 * BLK)
        self.blocks = self.chunk // BLK
        self.chunks = span // self.chunk
        self.spans = (self.me, 2 * shards - 1 - self.me)
        row_in = lax.broadcasted_iota(jnp.int32, (BLK, BLK), 0)
        col_in = lax.broadcasted_iota(jnp.int32, (BLK, BLK), 1)
        self.triangle = jnp.where(col_in <= row_in, 0.0, MASKED).astype(jnp.float32)

    def query_block(self, t, query_chunk):
        return self.spans[t] * self.per_span + query_chunk * self.blocks

    def tile(self, t, query_chunk, source, key_block, key_blocks, diagonal=False, o_ref=None):
        keys, key_row, values, value_row = source
        key_rows = pl.ds(pl.multiple_of(key_row, BLK), key_blocks * BLK)
        value_rows = pl.ds(pl.multiple_of(value_row, BLK), key_blocks * BLK)
        rows = pl.ds(pl.multiple_of(t * self.span + query_chunk * self.chunk, BLK), self.chunk)
        query_block = self.query_block(t, query_chunk)
        bias = {}
        for a in range(self.blocks):
            for c in range(key_blocks):
                same = self.doc_ref[query_block + a] == self.doc_ref[key_block + c]
                if diagonal and c > a:
                    same = jnp.bool_(False)
                bias[a, c] = jnp.where(same, 0.0, MASKED).astype(jnp.float32)
        key = keys[key_rows, :]
        ones = jnp.ones((key_blocks * BLK, HD), jnp.bfloat16)
        value = jnp.concatenate([values[value_rows, :], ones], axis=1)
        for h in range(self.heads):
            query = self.q_ref[rows, h * HD : (h + 1) * HD]
            scores = lax.dot_general(
                query, key, (((1,), (1,)), ((), ())), preferred_element_type=jnp.float32
            )
            lines, peaks = [], []
            for a in range(self.blocks):
                line = []
                for c in range(key_blocks):
                    part = scores[a * BLK : (a + 1) * BLK, c * BLK : (c + 1) * BLK]
                    part = part + bias[a, c]
                    if diagonal and a == c:
                        part = part + self.triangle
                    line.append(part)
                top = line[0]
                for part in line[1:]:
                    top = jnp.maximum(top, part)
                peaks.append(jnp.broadcast_to(jnp.max(top, axis=1, keepdims=True), (BLK, HD)))
                lines.append(line)
            peak = jnp.concatenate(peaks, axis=0)
            if not diagonal:
                before = self.m_ref[h, rows, :]
                peak = jnp.maximum(peak, before)
            weights = jnp.concatenate(
                [
                    jnp.concatenate(
                        [
                            jnp.exp2((part - peak[a * BLK : (a + 1) * BLK]) * SCALE2)
                            for part in line
                        ],
                        axis=1,
                    )
                    for a, line in enumerate(lines)
                ],
                axis=0,
            ).astype(jnp.bfloat16)
            mixed = jnp.dot(weights, value, preferred_element_type=jnp.float32)
            if not diagonal:
                shrink = jnp.exp2((before - peak) * SCALE2)
                mixed = mixed + self.acc_ref[h, rows, :] * jnp.concatenate([shrink, shrink], axis=1)
            if o_ref is None:
                self.m_ref[h, rows, :] = peak
                self.acc_ref[h, rows, :] = mixed
            else:
                o_ref[rows, h * HD : (h + 1) * HD] = normalised(mixed)

    def reaches(self, t, query_chunk, key_block, key_blocks):
        last = self.doc_ref[key_block + key_blocks - 1]
        return last == self.doc_ref[self.query_block(t, query_chunk)]

    def earlier(self, t, query_chunk, source, key_block, key_blocks, valid=True):
        @pl.when(self.reaches(t, query_chunk, key_block, key_blocks) & valid)
        def _():
            self.tile(t, query_chunk, source, key_block, key_blocks)

    def whole_span(self, t, source, key_span, valid=True):
        keys, key_row, values, value_row = source

        def step(index, carry):
            query_chunk, key_chunk = index // self.chunks, index % self.chunks
            row = key_chunk * self.chunk
            self.earlier(
                t,
                query_chunk,
                (keys, key_row + row, values, value_row + row),
                key_span * self.per_span + key_chunk * self.blocks,
                self.blocks,
                valid,
            )
            return carry

        if self.chunks == 1:
            step(0, 0)
        else:
            lax.fori_loop(0, self.chunks * self.chunks, step, 0)

    def local(self, own, key_row, value_row):
        for t in range(2):

            def step(index, carry, t=t):
                def source(chunk):
                    row = t * self.span + chunk * self.chunk
                    return own, key_row + row, own, value_row + row

                self.tile(
                    t, index, source(index), self.query_block(t, index), self.blocks, diagonal=True
                )

                def before(key_chunk, inner):
                    key_block = self.query_block(t, key_chunk)
                    self.earlier(t, index, source(key_chunk), key_block, self.blocks)
                    return inner

                if self.chunks > 1:
                    lax.fori_loop(0, index, before, 0)
                return carry

            if self.chunks == 1:
                step(0, 0)
            else:
                lax.fori_loop(0, self.chunks, step, 0)
        self.whole_span(1, (own, key_row, own, value_row), self.spans[0])

    def finish(self, t, o_ref):
        rows = pl.ds(t * self.span, self.span)
        for h in range(self.heads):
            o_ref[rows, h * HD : (h + 1) * HD] = normalised(self.acc_ref[h, rows, :])


def gathered_kernel(shards, q_ref, own, doc_ref, all_k, all_v, o_ref, m_ref, acc_ref):
    span, heads = q_ref.shape[0] // 2, q_ref.shape[1] // HD
    tiles = Tiles(shards, span, heads, q_ref, doc_ref, m_ref, acc_ref)
    tiles.local(own, 0, 2 * span)
    for t in range(2):

        def span_step(s, carry, t=t):
            holder = jnp.minimum(s, 2 * shards - 1 - s)
            row = (2 * holder + jnp.where(s < shards, 0, 1)) * span
            other = (s != tiles.spans[0]) if t == 1 else True
            tiles.whole_span(t, (all_k, row, all_v, row), s, other)
            return carry

        lax.fori_loop(0, tiles.spans[t], span_step, 0)
        tiles.finish(t, o_ref)


def partner_span(tiles, shards, r):
    partner = tiles.me ^ r
    return jnp.where(partner < tiles.me, partner, 2 * shards - 1 - partner)


def crosses(doc_ref, per_span):
    return doc_ref[4 * per_span - 1] == doc_ref[6 * per_span]


def reads_last(tiles, shards, t):
    key_span = partner_span(tiles, shards, 3)
    reaches = tiles.reaches(t, 0, key_span * tiles.per_span, tiles.blocks)
    return reaches & (key_span < tiles.spans[t])


def local_kernel(shards, q_hbm, own, doc_ref, q_ref, m_ref, acc_ref, sem):
    heads = q_ref.shape[1] // HD
    span = q_ref.shape[0] // 2
    fetch = pltpu.make_async_copy(q_hbm, q_ref, sem)
    fetch.start()
    fetch.wait()
    Tiles(shards, span, heads, q_ref, doc_ref, m_ref, acc_ref).local(own, 0, 2 * span)


def middle_kernel(shards, q_ref, doc_ref, m_in, acc_in, from2, from1, fix1, fix0, *refs):
    m_ref, acc_ref, o_ref = refs
    heads = q_ref.shape[1] // HD
    span = q_ref.shape[0] // 2
    half = span // 2
    before = Tiles(shards, span, heads, q_ref, doc_ref, m_in, acc_in)
    tiles = Tiles(shards, span, heads, q_ref, doc_ref, m_ref, acc_ref)
    me, per_span, blocks = tiles.me, tiles.per_span, tiles.blocks
    for t in range(2):
        sources = []
        for r, ref in ((2, from2), (1, from1)):
            key_span = partner_span(tiles, shards, r)
            source = (ref, 0, ref, span)
            sources.append((source, key_span * per_span, blocks, key_span < tiles.spans[t]))
        if t == 1:
            half_blocks = half // BLK
            block = jnp.where(me == 0, 3, 2) * per_span + per_span - half_blocks
            middle = (me == 1) | (me == 2)
            sources.append(((fix1, 0, fix1, span), 3 * per_span, blocks, middle))
            sources.append(((fix0, 0, fix0, half), block, half_blocks, me < 2))
        reads = [tiles.reaches(t, 0, block, count) & valid for _, block, count, valid in sources]
        more = reads_last(tiles, shards, t)
        changes = more
        for read in reads:
            changes = changes | read

        @pl.when(changes)
        def _(t=t):
            rows = pl.ds(t * span, span)
            m_ref[:, rows, :] = m_in[:, rows, :]
            acc_ref[:, rows, :] = acc_in[:, rows, :]

        for read, (source, block, count, _) in zip(reads, sources):

            @pl.when(read)
            def _(t=t, source=source, block=block, count=count):
                tiles.tile(t, 0, source, block, count)

        @pl.when(changes & jnp.logical_not(more))
        def _(t=t):
            tiles.finish(t, o_ref)

        @pl.when(jnp.logical_not(changes))
        def _(t=t):
            before.finish(t, o_ref)


def last_kernel(shards, q_ref, doc_ref, m_ref, acc_ref, part_ref, from3, o_hbm, o_ref, sems):
    heads = q_ref.shape[1] // HD
    span = q_ref.shape[0] // 2
    tiles = Tiles(shards, span, heads, q_ref, doc_ref, m_ref, acc_ref)
    key_block = partner_span(tiles, shards, 3) * tiles.per_span
    reads = [reads_last(tiles, shards, t) for t in range(2)]

    def copy(t, source):
        rows = pl.ds(t * span, span)
        return pltpu.make_async_copy(source.at[rows], o_hbm.at[rows], sems.at[t])

    for t in range(2):

        @pl.when(jnp.logical_not(reads[t]))
        def _(t=t):
            copy(t, part_ref).start()

    for t in range(2):

        @pl.when(reads[t])
        def _(t=t):
            tiles.tile(t, 0, (from3, 0, from3, span), key_block, tiles.blocks, o_ref=o_ref)
            copy(t, o_ref).start()

    for t in range(2):
        copy(t, o_ref).wait()


def plan_kernel(doc_ref, plan_ref):
    per_span = doc_ref.shape[0] // 8
    beside = doc_ref[4 * per_span - 1] == doc_ref[5 * per_span]
    plan_ref[0] = jnp.where(crosses(doc_ref, per_span), 2, jnp.where(beside, 1, 0))


def body(queries, keys, values, doc_blocks):
    shards = lax.axis_size("ctx")
    rows, heads = queries.shape[0], queries.shape[1] // HD
    span = rows // 2
    params = pltpu.CompilerParams(vmem_limit_bytes=16 * 1024 * 1024)
    state_shapes = [
        jax.ShapeDtypeStruct((heads, rows, HD), jnp.float32),
        jax.ShapeDtypeStruct((heads, rows, 2 * HD), jnp.float32),
    ]
    state_scratch = [pltpu.VMEM(x.shape, x.dtype) for x in state_shapes]
    out_shape = jax.ShapeDtypeStruct(queries.shape, jnp.bfloat16)

    if shards != 4:
        received = [lax.all_gather(x, "ctx", axis=0, tiled=True) for x in (keys, values)]
        return pl.pallas_call(
            lambda *refs: gathered_kernel(shards, *refs),
            in_specs=[VMEM, VMEM, SMEM, VMEM, VMEM],
            out_specs=VMEM,
            out_shape=out_shape,
            scratch_shapes=state_scratch,
            compiler_params=params,
            name="attend",
        )(queries, jnp.concatenate([keys, values]), doc_blocks, *received)

    me = lax.axis_index("ctx")

    def swap(array, r):
        return lax.ppermute(array, "ctx", [(i, i ^ r) for i in range(shards)])

    def send(array, *pairs):
        return lax.ppermute(array, "ctx", pairs)

    own = lax.optimization_barrier(jnp.concatenate([keys, values], axis=0))

    def span_for(r, own):
        row = jnp.where((me ^ r) > me, 0, span)
        parts = [lax.dynamic_slice_in_dim(own, row + base, span, 0) for base in (0, rows)]
        return jnp.concatenate(parts, axis=0)

    def lower_rows(start):
        return jnp.concatenate([own[start:span], own[rows + start : rows + span]], axis=0)

    far = span_for(2, own)
    far, own = lax.optimization_barrier((far, own))
    near, lower, half = span_for(1, own), lower_rows(0), lower_rows(span // 2)
    from2, from1, from3 = swap(far, 2), swap(near, 1), swap(far, 3)
    plan = pl.pallas_call(
        plan_kernel,
        in_specs=[SMEM],
        out_specs=SMEM,
        out_shape=jax.ShapeDtypeStruct((1,), jnp.int32),
        name="plan",
    )(doc_blocks)

    def narrow(lower, half):
        return lower, half

    def beside(lower, half):
        return send(lower, (3, 2)), half

    def crossing(lower, half):
        fix1, fix0 = send(lower, (3, 1)), send(half, (3, 0), (2, 1))
        return fix1 + send(lower, (3, 2)), fix0

    fixes = lax.switch(plan[0], [narrow, beside, crossing], lower, half)
    q, m, acc = pl.pallas_call(
        lambda *refs: local_kernel(shards, *refs),
        in_specs=[ANY, VMEM, SMEM],
        out_specs=[VMEM] * 3,
        out_shape=[out_shape] + state_shapes,
        scratch_shapes=[pltpu.SemaphoreType.DMA],
        compiler_params=params,
        name="local",
    )(queries, own, doc_blocks)
    m, acc, part = pl.pallas_call(
        lambda *refs: middle_kernel(shards, *refs),
        in_specs=[VMEM, SMEM] + [VMEM] * 6,
        out_specs=[VMEM] * 3,
        out_shape=state_shapes + [out_shape],
        compiler_params=params,
        name="middle",
    )(q, doc_blocks, m, acc, from2, from1, *fixes)
    return pl.pallas_call(
        lambda *refs: last_kernel(shards, *refs),
        in_specs=[VMEM, SMEM] + [VMEM] * 4,
        out_specs=ANY,
        out_shape=out_shape,
        scratch_shapes=[
            pltpu.VMEM(out_shape.shape, out_shape.dtype),
            pltpu.SemaphoreType.DMA((2,)),
        ],
        compiler_params=params,
        name="last",
    )(q, doc_blocks, m, acc, part, from3)


def solution(mesh):
    return jax.shard_map(
        body,
        mesh=mesh,
        in_specs=(P("ctx", "tp"), P("ctx", "tp"), P("ctx", "tp"), P()),
        out_specs=P("ctx", "tp"),
        check_vma=False,
    )
```

```python
import math

import jax
import jax.numpy as jnp
from jax import lax
from jax.experimental import pallas as pl
from jax.experimental.pallas import tpu as pltpu
from jax.sharding import PartitionSpec as P

HD = 128
BLK = 128
MASKED = -1e30
SCALE2 = HD ** (-0.5) * math.log2(math.e)
VMEM = pl.BlockSpec(memory_space=pltpu.VMEM)
SMEM = pl.BlockSpec(memory_space=pltpu.SMEM)


ANY = pl.BlockSpec(memory_space=pl.ANY)


def normalised(mixed):
    inverse = pl.reciprocal(mixed[:, HD:], approx=True)
    inverse = inverse * (2.0 - mixed[:, HD:] * inverse)
    return (mixed[:, :HD] * inverse).astype(jnp.bfloat16)


class Tiles:
    def __init__(self, shards, span, heads, q_ref, doc_ref, m_ref, acc_ref):
        self.span, self.heads = span, heads
        self.q_ref, self.doc_ref, self.m_ref, self.acc_ref = q_ref, doc_ref, m_ref, acc_ref
        self.me = lax.axis_index("ctx")
        self.per_span = span // BLK
        self.chunk = min(span, 2 * BLK)
        self.blocks = self.chunk // BLK
        self.chunks = span // self.chunk
        self.spans = (self.me, 2 * shards - 1 - self.me)
        row_in = lax.broadcasted_iota(jnp.int32, (BLK, BLK), 0)
        col_in = lax.broadcasted_iota(jnp.int32, (BLK, BLK), 1)
        self.triangle = jnp.where(col_in <= row_in, 0.0, MASKED).astype(jnp.float32)

    def query_block(self, t, query_chunk):
        return self.spans[t] * self.per_span + query_chunk * self.blocks

    def tile(self, t, query_chunk, source, key_block, key_blocks, diagonal=False, o_ref=None):
        keys, key_row, values, value_row = source
        key_rows = pl.ds(pl.multiple_of(key_row, BLK), key_blocks * BLK)
        value_rows = pl.ds(pl.multiple_of(value_row, BLK), key_blocks * BLK)
        rows = pl.ds(pl.multiple_of(t * self.span + query_chunk * self.chunk, BLK), self.chunk)
        query_block = self.query_block(t, query_chunk)
        bias = {}
        for a in range(self.blocks):
            for c in range(key_blocks):
                same = self.doc_ref[query_block + a] == self.doc_ref[key_block + c]
                if diagonal and c > a:
                    same = jnp.bool_(False)
                bias[a, c] = jnp.where(same, 0.0, MASKED).astype(jnp.float32)
        key = keys[key_rows, :]
        ones = jnp.ones((key_blocks * BLK, HD), jnp.bfloat16)
        value = jnp.concatenate([values[value_rows, :], ones], axis=1)
        for h in range(self.heads):
            query = self.q_ref[rows, h * HD : (h + 1) * HD]
            scores = lax.dot_general(
                query, key, (((1,), (1,)), ((), ())), preferred_element_type=jnp.float32
            )
            lines, peaks = [], []
            for a in range(self.blocks):
                line = []
                for c in range(key_blocks):
                    part = scores[a * BLK : (a + 1) * BLK, c * BLK : (c + 1) * BLK]
                    part = part + bias[a, c]
                    if diagonal and a == c:
                        part = part + self.triangle
                    line.append(part)
                top = line[0]
                for part in line[1:]:
                    top = jnp.maximum(top, part)
                peaks.append(jnp.broadcast_to(jnp.max(top, axis=1, keepdims=True), (BLK, HD)))
                lines.append(line)
            peak = jnp.concatenate(peaks, axis=0)
            if not diagonal:
                before = self.m_ref[h, rows, :]
                peak = jnp.maximum(peak, before)
            weights = jnp.concatenate(
                [
                    jnp.concatenate(
                        [
                            jnp.exp2((part - peak[a * BLK : (a + 1) * BLK]) * SCALE2)
                            for part in line
                        ],
                        axis=1,
                    )
                    for a, line in enumerate(lines)
                ],
                axis=0,
            ).astype(jnp.bfloat16)
            mixed = jnp.dot(weights, value, preferred_element_type=jnp.float32)
            if not diagonal:
                shrink = jnp.exp2((before - peak) * SCALE2)
                mixed = mixed + self.acc_ref[h, rows, :] * jnp.concatenate([shrink, shrink], axis=1)
            if o_ref is None:
                self.m_ref[h, rows, :] = peak
                self.acc_ref[h, rows, :] = mixed
            else:
                o_ref[rows, h * HD : (h + 1) * HD] = normalised(mixed)

    def reaches(self, t, query_chunk, key_block, key_blocks):
        last = self.doc_ref[key_block + key_blocks - 1]
        return last == self.doc_ref[self.query_block(t, query_chunk)]

    def earlier(self, t, query_chunk, source, key_block, key_blocks, valid=True):
        @pl.when(self.reaches(t, query_chunk, key_block, key_blocks) & valid)
        def _():
            self.tile(t, query_chunk, source, key_block, key_blocks)

    def whole_span(self, t, source, key_span, valid=True):
        keys, key_row, values, value_row = source

        def step(index, carry):
            query_chunk, key_chunk = index // self.chunks, index % self.chunks
            row = key_chunk * self.chunk
            self.earlier(
                t,
                query_chunk,
                (keys, key_row + row, values, value_row + row),
                key_span * self.per_span + key_chunk * self.blocks,
                self.blocks,
                valid,
            )
            return carry

        if self.chunks == 1:
            step(0, 0)
        else:
            lax.fori_loop(0, self.chunks * self.chunks, step, 0)

    def local(self, own, key_row, value_row):
        for t in range(2):

            def step(index, carry, t=t):
                def source(chunk):
                    row = t * self.span + chunk * self.chunk
                    return own, key_row + row, own, value_row + row

                self.tile(
                    t, index, source(index), self.query_block(t, index), self.blocks, diagonal=True
                )

                def before(key_chunk, inner):
                    key_block = self.query_block(t, key_chunk)
                    self.earlier(t, index, source(key_chunk), key_block, self.blocks)
                    return inner

                if self.chunks > 1:
                    lax.fori_loop(0, index, before, 0)
                return carry

            if self.chunks == 1:
                step(0, 0)
            else:
                lax.fori_loop(0, self.chunks, step, 0)
        self.whole_span(1, (own, key_row, own, value_row), self.spans[0])

    def finish(self, t, o_ref):
        rows = pl.ds(t * self.span, self.span)
        for h in range(self.heads):
            o_ref[rows, h * HD : (h + 1) * HD] = normalised(self.acc_ref[h, rows, :])


def gathered_kernel(shards, q_ref, own, doc_ref, all_k, all_v, o_ref, m_ref, acc_ref):
    span, heads = q_ref.shape[0] // 2, q_ref.shape[1] // HD
    tiles = Tiles(shards, span, heads, q_ref, doc_ref, m_ref, acc_ref)
    tiles.local(own, 0, 2 * span)
    for t in range(2):

        def span_step(s, carry, t=t):
            holder = jnp.minimum(s, 2 * shards - 1 - s)
            row = (2 * holder + jnp.where(s < shards, 0, 1)) * span
            other = (s != tiles.spans[0]) if t == 1 else True
            tiles.whole_span(t, (all_k, row, all_v, row), s, other)
            return carry

        lax.fori_loop(0, tiles.spans[t], span_step, 0)
        tiles.finish(t, o_ref)


def partner_span(tiles, shards, r):
    partner = tiles.me ^ r
    return jnp.where(partner < tiles.me, partner, 2 * shards - 1 - partner)


def reads_last(tiles, shards, t):
    key_span = partner_span(tiles, shards, 3)
    reaches = tiles.reaches(t, 0, key_span * tiles.per_span, tiles.blocks)
    return reaches & (key_span < tiles.spans[t])


def local_kernel(shards, q_hbm, own, doc_ref, q_ref, m_ref, acc_ref, sem):
    heads = q_ref.shape[1] // HD
    span = q_ref.shape[0] // 2
    fetch = pltpu.make_async_copy(q_hbm, q_ref, sem)
    fetch.start()
    fetch.wait()
    Tiles(shards, span, heads, q_ref, doc_ref, m_ref, acc_ref).local(own, 0, 2 * span)


def middle_kernel(shards, q_ref, doc_ref, m_in, acc_in, from2, from1, fix1, fix0, *refs):
    m_ref, acc_ref, o_ref = refs
    heads = q_ref.shape[1] // HD
    span = q_ref.shape[0] // 2
    half = span // 2
    before = Tiles(shards, span, heads, q_ref, doc_ref, m_in, acc_in)
    tiles = Tiles(shards, span, heads, q_ref, doc_ref, m_ref, acc_ref)
    me, per_span, blocks = tiles.me, tiles.per_span, tiles.blocks
    for t in range(2):
        sources = []
        for r, ref in ((2, from2), (1, from1)):
            key_span = partner_span(tiles, shards, r)
            source = (ref, 0, ref, span)
            sources.append((source, key_span * per_span, blocks, key_span < tiles.spans[t]))
        if t == 1:
            half_blocks = half // BLK
            block = jnp.where(me == 0, 3, 2) * per_span + per_span - half_blocks
            middle = (me == 1) | (me == 2)
            sources.append(((fix1, 0, fix1, span), 3 * per_span, blocks, middle))
            sources.append(((fix0, 0, fix0, half), block, half_blocks, me < 2))
        reads = [tiles.reaches(t, 0, block, count) & valid for _, block, count, valid in sources]
        more = reads_last(tiles, shards, t)
        changes = more
        for read in reads:
            changes = changes | read

        @pl.when(changes)
        def _(t=t):
            rows = pl.ds(t * span, span)
            m_ref[:, rows, :] = m_in[:, rows, :]
            acc_ref[:, rows, :] = acc_in[:, rows, :]

        for read, (source, block, count, _) in zip(reads, sources):

            @pl.when(read)
            def _(t=t, source=source, block=block, count=count):
                tiles.tile(t, 0, source, block, count)

        @pl.when(changes & jnp.logical_not(more))
        def _(t=t):
            tiles.finish(t, o_ref)

        @pl.when(jnp.logical_not(changes))
        def _(t=t):
            before.finish(t, o_ref)


def last_kernel(shards, q_ref, doc_ref, m_ref, acc_ref, part_ref, from3, o_hbm, o_ref, sems):
    heads = q_ref.shape[1] // HD
    span = q_ref.shape[0] // 2
    tiles = Tiles(shards, span, heads, q_ref, doc_ref, m_ref, acc_ref)
    key_block = partner_span(tiles, shards, 3) * tiles.per_span
    reads = [reads_last(tiles, shards, t) for t in range(2)]

    def copy(t, source):
        rows = pl.ds(t * span, span)
        return pltpu.make_async_copy(source.at[rows], o_hbm.at[rows], sems.at[t])

    for t in range(2):

        @pl.when(jnp.logical_not(reads[t]))
        def _(t=t):
            copy(t, part_ref).start()

    for t in range(2):

        @pl.when(reads[t])
        def _(t=t):
            tiles.tile(t, 0, (from3, 0, from3, span), key_block, tiles.blocks, o_ref=o_ref)
            copy(t, o_ref).start()

    for t in range(2):
        copy(t, o_ref).wait()


def plan_kernel(doc_ref, plan_ref):
    per_span = doc_ref.shape[0] // 8

    def reads(t, s):
        return doc_ref[(s + 1) * per_span - 1] == doc_ref[t * per_span]

    across = jnp.where(reads(6, 2), 3, jnp.where(reads(7, 3), 4, 2))
    plan_ref[0] = jnp.where(reads(6, 3), across, jnp.where(reads(5, 3), 1, 0))


def body(queries, keys, values, doc_blocks):
    shards = lax.axis_size("ctx")
    rows, heads = queries.shape[0], queries.shape[1] // HD
    span = rows // 2
    params = pltpu.CompilerParams(vmem_limit_bytes=16 * 1024 * 1024)
    state_shapes = [
        jax.ShapeDtypeStruct((heads, rows, HD), jnp.float32),
        jax.ShapeDtypeStruct((heads, rows, 2 * HD), jnp.float32),
    ]
    state_scratch = [pltpu.VMEM(x.shape, x.dtype) for x in state_shapes]
    out_shape = jax.ShapeDtypeStruct(queries.shape, jnp.bfloat16)

    if shards != 4:
        received = [lax.all_gather(x, "ctx", axis=0, tiled=True) for x in (keys, values)]
        return pl.pallas_call(
            lambda *refs: gathered_kernel(shards, *refs),
            in_specs=[VMEM, VMEM, SMEM, VMEM, VMEM],
            out_specs=VMEM,
            out_shape=out_shape,
            scratch_shapes=state_scratch,
            compiler_params=params,
            name="attend",
        )(queries, jnp.concatenate([keys, values]), doc_blocks, *received)

    me = lax.axis_index("ctx")

    def swap(array, r):
        return lax.ppermute(array, "ctx", [(i, i ^ r) for i in range(shards)])

    def send(array, *pairs):
        return lax.ppermute(array, "ctx", pairs)

    own = lax.optimization_barrier(jnp.concatenate([keys, values], axis=0))

    def span_for(r, own):
        row = jnp.where((me ^ r) > me, 0, span)
        parts = [lax.dynamic_slice_in_dim(own, row + base, span, 0) for base in (0, rows)]
        return jnp.concatenate(parts, axis=0)

    def lower_rows(start):
        return jnp.concatenate([own[start:span], own[rows + start : rows + span]], axis=0)

    far = span_for(2, own)
    far, own = lax.optimization_barrier((far, own))
    near, lower, half = span_for(1, own), lower_rows(0), lower_rows(span // 2)
    from2, from1, from3 = swap(far, 2), swap(near, 1), swap(far, 3)
    plan = pl.pallas_call(
        plan_kernel,
        in_specs=[SMEM],
        out_specs=SMEM,
        out_shape=jax.ShapeDtypeStruct((1,), jnp.int32),
        name="plan",
    )(doc_blocks)

    def narrow(lower, half):
        return lower, half

    def beside(lower, half):
        return send(lower, (3, 2)), half

    def across(lower, half):
        return send(lower, (3, 1)) + send(lower, (3, 2)), half

    def across_from_2(lower, half):
        fix1 = send(lower, (3, 1))
        fix0 = send(half, (2, 1))
        return fix1 + send(lower, (3, 2)), fix0

    def across_to_7(lower, half):
        fix1, fix0 = send(half, (3, 1)), send(half, (3, 0))
        second = fix1 + send(half, (3, 2))
        blank = jnp.zeros_like(second[: span // 2])
        parts = [blank, second[: span // 2], blank, second[span // 2 :]]
        return jnp.concatenate(parts, axis=0), fix0

    branches = [narrow, beside, across, across_from_2, across_to_7]
    fixes = lax.switch(plan[0], branches, lower, half)
    q, m, acc = pl.pallas_call(
        lambda *refs: local_kernel(shards, *refs),
        in_specs=[ANY, VMEM, SMEM],
        out_specs=[VMEM] * 3,
        out_shape=[out_shape] + state_shapes,
        scratch_shapes=[pltpu.SemaphoreType.DMA],
        compiler_params=params,
        name="local",
    )(queries, own, doc_blocks)
    m, acc, part = pl.pallas_call(
        lambda *refs: middle_kernel(shards, *refs),
        in_specs=[VMEM, SMEM] + [VMEM] * 6,
        out_specs=[VMEM] * 3,
        out_shape=state_shapes + [out_shape],
        compiler_params=params,
        name="middle",
    )(q, doc_blocks, m, acc, from2, from1, *fixes)
    return pl.pallas_call(
        lambda *refs: last_kernel(shards, *refs),
        in_specs=[VMEM, SMEM] + [VMEM] * 4,
        out_specs=ANY,
        out_shape=out_shape,
        scratch_shapes=[
            pltpu.VMEM(out_shape.shape, out_shape.dtype),
            pltpu.SemaphoreType.DMA((2,)),
        ],
        compiler_params=params,
        name="last",
    )(q, doc_blocks, m, acc, part, from3)


def solution(mesh):
    return jax.shard_map(
        body,
        mesh=mesh,
        in_specs=(P("ctx", "tp"), P("ctx", "tp"), P("ctx", "tp"), P()),
        out_specs=P("ctx", "tp"),
        check_vma=False,
    )
```

```python
import math

import jax
import jax.numpy as jnp
from jax import lax
from jax.experimental import pallas as pl
from jax.experimental.pallas import tpu as pltpu
from jax.sharding import PartitionSpec as P

HD = 128
BLK = 128
MASKED = -1e30
SCALE2 = HD ** (-0.5) * math.log2(math.e)
VMEM = pl.BlockSpec(memory_space=pltpu.VMEM)
SMEM = pl.BlockSpec(memory_space=pltpu.SMEM)


ANY = pl.BlockSpec(memory_space=pl.ANY)


def normalised(mixed):
    inverse = pl.reciprocal(mixed[:, HD:], approx=True)
    inverse = inverse * (2.0 - mixed[:, HD:] * inverse)
    return (mixed[:, :HD] * inverse).astype(jnp.bfloat16)


class Tiles:
    def __init__(self, shards, span, heads, q_ref, doc_ref, m_ref, acc_ref):
        self.span, self.heads = span, heads
        self.q_ref, self.doc_ref, self.m_ref, self.acc_ref = q_ref, doc_ref, m_ref, acc_ref
        self.me = lax.axis_index("ctx")
        self.per_span = span // BLK
        self.chunk = min(span, 2 * BLK)
        self.blocks = self.chunk // BLK
        self.chunks = span // self.chunk
        self.spans = (self.me, 2 * shards - 1 - self.me)
        row_in = lax.broadcasted_iota(jnp.int32, (BLK, BLK), 0)
        col_in = lax.broadcasted_iota(jnp.int32, (BLK, BLK), 1)
        self.triangle = jnp.where(col_in <= row_in, 0.0, MASKED).astype(jnp.float32)

    def query_block(self, t, query_chunk):
        return self.spans[t] * self.per_span + query_chunk * self.blocks

    def tile(self, t, query_chunk, source, key_block, key_blocks, diagonal=False, o_ref=None, send=None):
        keys, key_row, values, value_row = source
        key_rows = pl.ds(pl.multiple_of(key_row, BLK), key_blocks * BLK)
        value_rows = pl.ds(pl.multiple_of(value_row, BLK), key_blocks * BLK)
        rows = pl.ds(pl.multiple_of(t * self.span + query_chunk * self.chunk, BLK), self.chunk)
        query_block = self.query_block(t, query_chunk)
        bias = {}
        for a in range(self.blocks):
            for c in range(key_blocks):
                same = self.doc_ref[query_block + a] == self.doc_ref[key_block + c]
                if diagonal and c > a:
                    same = jnp.bool_(False)
                bias[a, c] = jnp.where(same, 0.0, MASKED).astype(jnp.float32)
        key = keys[key_rows, :]
        ones = jnp.ones((key_blocks * BLK, HD), jnp.bfloat16)
        value = jnp.concatenate([values[value_rows, :], ones], axis=1)
        for h in range(self.heads):
            query = self.q_ref[rows, h * HD : (h + 1) * HD]
            scores = lax.dot_general(
                query, key, (((1,), (1,)), ((), ())), preferred_element_type=jnp.float32
            )
            lines, peaks = [], []
            for a in range(self.blocks):
                line = []
                for c in range(key_blocks):
                    part = scores[a * BLK : (a + 1) * BLK, c * BLK : (c + 1) * BLK]
                    part = part + bias[a, c]
                    if diagonal and a == c:
                        part = part + self.triangle
                    line.append(part)
                top = line[0]
                for part in line[1:]:
                    top = jnp.maximum(top, part)
                peaks.append(jnp.broadcast_to(jnp.max(top, axis=1, keepdims=True), (BLK, HD)))
                lines.append(line)
            peak = jnp.concatenate(peaks, axis=0)
            if not diagonal:
                before = self.m_ref[h, rows, :]
                peak = jnp.maximum(peak, before)
            weights = jnp.concatenate(
                [
                    jnp.concatenate(
                        [
                            jnp.exp2((part - peak[a * BLK : (a + 1) * BLK]) * SCALE2)
                            for part in line
                        ],
                        axis=1,
                    )
                    for a, line in enumerate(lines)
                ],
                axis=0,
            ).astype(jnp.bfloat16)
            mixed = jnp.dot(weights, value, preferred_element_type=jnp.float32)
            if not diagonal:
                shrink = jnp.exp2((before - peak) * SCALE2)
                mixed = mixed + self.acc_ref[h, rows, :] * jnp.concatenate([shrink, shrink], axis=1)
            if o_ref is None:
                self.m_ref[h, rows, :] = peak
                self.acc_ref[h, rows, :] = mixed
            else:
                o_ref[rows, h * HD : (h + 1) * HD] = normalised(mixed)
                send(t, h).start()

    def reaches(self, t, query_chunk, key_block, key_blocks):
        last = self.doc_ref[key_block + key_blocks - 1]
        return last == self.doc_ref[self.query_block(t, query_chunk)]

    def earlier(self, t, query_chunk, source, key_block, key_blocks, valid=True):
        @pl.when(self.reaches(t, query_chunk, key_block, key_blocks) & valid)
        def _():
            self.tile(t, query_chunk, source, key_block, key_blocks)

    def whole_span(self, t, source, key_span, valid=True):
        keys, key_row, values, value_row = source

        def step(index, carry):
            query_chunk, key_chunk = index // self.chunks, index % self.chunks
            row = key_chunk * self.chunk
            self.earlier(
                t,
                query_chunk,
                (keys, key_row + row, values, value_row + row),
                key_span * self.per_span + key_chunk * self.blocks,
                self.blocks,
                valid,
            )
            return carry

        if self.chunks == 1:
            step(0, 0)
        else:
            lax.fori_loop(0, self.chunks * self.chunks, step, 0)

    def local(self, own, key_row, value_row):
        for t in range(2):

            def step(index, carry, t=t):
                def source(chunk):
                    row = t * self.span + chunk * self.chunk
                    return own, key_row + row, own, value_row + row

                self.tile(
                    t, index, source(index), self.query_block(t, index), self.blocks, diagonal=True
                )

                def before(key_chunk, inner):
                    key_block = self.query_block(t, key_chunk)
                    self.earlier(t, index, source(key_chunk), key_block, self.blocks)
                    return inner

                if self.chunks > 1:
                    lax.fori_loop(0, index, before, 0)
                return carry

            if self.chunks == 1:
                step(0, 0)
            else:
                lax.fori_loop(0, self.chunks, step, 0)
        self.whole_span(1, (own, key_row, own, value_row), self.spans[0])

    def finish(self, t, o_ref):
        rows = pl.ds(t * self.span, self.span)
        for h in range(self.heads):
            o_ref[rows, h * HD : (h + 1) * HD] = normalised(self.acc_ref[h, rows, :])


def gathered_kernel(shards, q_ref, own, doc_ref, all_k, all_v, o_ref, m_ref, acc_ref):
    span, heads = q_ref.shape[0] // 2, q_ref.shape[1] // HD
    tiles = Tiles(shards, span, heads, q_ref, doc_ref, m_ref, acc_ref)
    tiles.local(own, 0, 2 * span)
    for t in range(2):

        def span_step(s, carry, t=t):
            holder = jnp.minimum(s, 2 * shards - 1 - s)
            row = (2 * holder + jnp.where(s < shards, 0, 1)) * span
            other = (s != tiles.spans[0]) if t == 1 else True
            tiles.whole_span(t, (all_k, row, all_v, row), s, other)
            return carry

        lax.fori_loop(0, tiles.spans[t], span_step, 0)
        tiles.finish(t, o_ref)


def partner_span(tiles, shards, r):
    partner = tiles.me ^ r
    return jnp.where(partner < tiles.me, partner, 2 * shards - 1 - partner)


def reads_last(tiles, shards, t):
    key_span = partner_span(tiles, shards, 3)
    reaches = tiles.reaches(t, 0, key_span * tiles.per_span, tiles.blocks)
    return reaches & (key_span < tiles.spans[t])


def local_kernel(shards, q_hbm, own, doc_ref, q_ref, m_ref, acc_ref, sem):
    heads = q_ref.shape[1] // HD
    span = q_ref.shape[0] // 2
    fetch = pltpu.make_async_copy(q_hbm, q_ref, sem)
    fetch.start()
    fetch.wait()
    Tiles(shards, span, heads, q_ref, doc_ref, m_ref, acc_ref).local(own, 0, 2 * span)


def middle_kernel(shards, q_ref, doc_ref, m_in, acc_in, from2, from1, fix1, fix0, *refs):
    m_ref, acc_ref, o_hbm, o_ref, sems = refs
    heads = q_ref.shape[1] // HD
    span = q_ref.shape[0] // 2
    half = span // 2
    finished = []
    before = Tiles(shards, span, heads, q_ref, doc_ref, m_in, acc_in)
    tiles = Tiles(shards, span, heads, q_ref, doc_ref, m_ref, acc_ref)
    me, per_span, blocks = tiles.me, tiles.per_span, tiles.blocks
    for t in range(2):
        sources = []
        for r, ref in ((2, from2), (1, from1)):
            key_span = partner_span(tiles, shards, r)
            source = (ref, 0, ref, span)
            sources.append((source, key_span * per_span, blocks, key_span < tiles.spans[t]))
        if t == 1:
            half_blocks = half // BLK
            block = jnp.where(me == 0, 3, 2) * per_span + per_span - half_blocks
            middle = (me == 1) | (me == 2)
            sources.append(((fix1, 0, fix1, span), 3 * per_span, blocks, middle))
            sources.append(((fix0, 0, fix0, half), block, half_blocks, me < 2))
        reads = [tiles.reaches(t, 0, block, count) & valid for _, block, count, valid in sources]
        more = reads_last(tiles, shards, t)
        changes = more
        for read in reads:
            changes = changes | read

        @pl.when(changes)
        def _(t=t):
            rows = pl.ds(t * span, span)
            m_ref[:, rows, :] = m_in[:, rows, :]
            acc_ref[:, rows, :] = acc_in[:, rows, :]

        for read, (source, block, count, _) in zip(reads, sources):

            @pl.when(read)
            def _(t=t, source=source, block=block, count=count):
                tiles.tile(t, 0, source, block, count)

        @pl.when(changes & jnp.logical_not(more))
        def _(t=t):
            tiles.finish(t, o_ref)

        @pl.when(jnp.logical_not(changes))
        def _(t=t):
            before.finish(t, o_ref)

        rows = pl.ds(t * span, span)
        copy = pltpu.make_async_copy(o_ref.at[rows], o_hbm.at[rows], sems.at[t])
        finished.append((jnp.logical_not(more), copy))

        @pl.when(jnp.logical_not(more))
        def _(copy=copy):
            copy.start()

    for condition, copy in finished:

        @pl.when(condition)
        def _(copy=copy):
            copy.wait()


def last_kernel(shards, q_ref, doc_ref, m_ref, acc_ref, from3, _, o_hbm, o_ref, sems):
    heads = q_ref.shape[1] // HD
    span = q_ref.shape[0] // 2
    tiles = Tiles(shards, span, heads, q_ref, doc_ref, m_ref, acc_ref)
    key_block = partner_span(tiles, shards, 3) * tiles.per_span
    reads = [reads_last(tiles, shards, t) for t in range(2)]

    def send(t, h):
        part = (pl.ds(t * span, span), pl.ds(h * HD, HD))
        return pltpu.make_async_copy(o_ref.at[part], o_hbm.at[part], sems.at[t, h])

    for t in range(2):

        @pl.when(reads[t])
        def _(t=t):
            source = (from3, 0, from3, span)
            tiles.tile(t, 0, source, key_block, tiles.blocks, o_ref=o_ref, send=send)

    for t in range(2):

        @pl.when(reads[t])
        def _(t=t):
            for h in range(heads):
                send(t, h).wait()


def plan_kernel(doc_ref, plan_ref):
    per_span = doc_ref.shape[0] // 8

    def reads(t, s):
        return doc_ref[(s + 1) * per_span - 1] == doc_ref[t * per_span]

    across = jnp.where(reads(6, 2), 3, jnp.where(reads(7, 3), 4, 2))
    plan_ref[0] = jnp.where(reads(6, 3), across, jnp.where(reads(5, 3), 1, 0))


def body(queries, keys, values, doc_blocks):
    shards = lax.axis_size("ctx")
    rows, heads = queries.shape[0], queries.shape[1] // HD
    span = rows // 2
    params = pltpu.CompilerParams(vmem_limit_bytes=16 * 1024 * 1024)
    state_shapes = [
        jax.ShapeDtypeStruct((heads, rows, HD), jnp.float32),
        jax.ShapeDtypeStruct((heads, rows, 2 * HD), jnp.float32),
    ]
    state_scratch = [pltpu.VMEM(x.shape, x.dtype) for x in state_shapes]
    out_shape = jax.ShapeDtypeStruct(queries.shape, jnp.bfloat16)

    if shards != 4:
        received = [lax.all_gather(x, "ctx", axis=0, tiled=True) for x in (keys, values)]
        return pl.pallas_call(
            lambda *refs: gathered_kernel(shards, *refs),
            in_specs=[VMEM, VMEM, SMEM, VMEM, VMEM],
            out_specs=VMEM,
            out_shape=out_shape,
            scratch_shapes=state_scratch,
            compiler_params=params,
            name="attend",
        )(queries, jnp.concatenate([keys, values]), doc_blocks, *received)

    me = lax.axis_index("ctx")

    def swap(array, r):
        return lax.ppermute(array, "ctx", [(i, i ^ r) for i in range(shards)])

    def send(array, *pairs):
        return lax.ppermute(array, "ctx", pairs)

    own = lax.optimization_barrier(jnp.concatenate([keys, values], axis=0))

    def span_for(r, own):
        row = jnp.where((me ^ r) > me, 0, span)
        parts = [lax.dynamic_slice_in_dim(own, row + base, span, 0) for base in (0, rows)]
        return jnp.concatenate(parts, axis=0)

    def lower_rows(start):
        return jnp.concatenate([own[start:span], own[rows + start : rows + span]], axis=0)

    far = span_for(2, own)
    far, own = lax.optimization_barrier((far, own))
    near, lower, half = span_for(1, own), lower_rows(0), lower_rows(span // 2)
    from2, from1, from3 = swap(far, 2), swap(near, 1), swap(far, 3)
    plan = pl.pallas_call(
        plan_kernel,
        in_specs=[SMEM],
        out_specs=SMEM,
        out_shape=jax.ShapeDtypeStruct((1,), jnp.int32),
        name="plan",
    )(doc_blocks)

    def narrow(lower, half):
        return lower, half

    def beside(lower, half):
        return send(lower, (3, 2)), half

    def across(lower, half):
        return send(lower, (3, 1)) + send(lower, (3, 2)), half

    def across_from_2(lower, half):
        fix1 = send(lower, (3, 1))
        fix0 = send(half, (2, 1))
        return fix1 + send(lower, (3, 2)), fix0

    def across_to_7(lower, half):
        fix1, fix0 = send(half, (3, 1)), send(half, (3, 0))
        second = fix1 + send(half, (3, 2))
        blank = jnp.zeros_like(second[: span // 2])
        parts = [blank, second[: span // 2], blank, second[span // 2 :]]
        return jnp.concatenate(parts, axis=0), fix0

    branches = [narrow, beside, across, across_from_2, across_to_7]
    fixes = lax.switch(plan[0], branches, lower, half)
    q, m, acc = pl.pallas_call(
        lambda *refs: local_kernel(shards, *refs),
        in_specs=[ANY, VMEM, SMEM],
        out_specs=[VMEM] * 3,
        out_shape=[out_shape] + state_shapes,
        scratch_shapes=[pltpu.SemaphoreType.DMA],
        compiler_params=params,
        name="local",
    )(queries, own, doc_blocks)
    m, acc, part = pl.pallas_call(
        lambda *refs: middle_kernel(shards, *refs),
        in_specs=[VMEM, SMEM] + [VMEM] * 6,
        out_specs=[VMEM, VMEM, ANY],
        out_shape=state_shapes + [out_shape],
        scratch_shapes=[
            pltpu.VMEM(out_shape.shape, out_shape.dtype),
            pltpu.SemaphoreType.DMA((2,)),
        ],
        compiler_params=params,
        name="middle",
    )(q, doc_blocks, m, acc, from2, from1, *fixes)
    return pl.pallas_call(
        lambda *refs: last_kernel(shards, *refs),
        in_specs=[VMEM, SMEM, VMEM, VMEM, VMEM, ANY],
        out_specs=ANY,
        out_shape=out_shape,
        input_output_aliases={5: 0},
        scratch_shapes=[
            pltpu.VMEM(out_shape.shape, out_shape.dtype),
            pltpu.SemaphoreType.DMA((2, heads)),
        ],
        compiler_params=params,
        name="last",
    )(q, doc_blocks, m, acc, from3, part)


def solution(mesh):
    return jax.shard_map(
        body,
        mesh=mesh,
        in_specs=(P("ctx", "tp"), P("ctx", "tp"), P("ctx", "tp"), P()),
        out_specs=P("ctx", "tp"),
        check_vma=False,
    )
```

```python
import math

import jax
import jax.numpy as jnp
from jax import lax
from jax.experimental import pallas as pl
from jax.experimental.pallas import tpu as pltpu
from jax.sharding import PartitionSpec as P

HD = 128
BLK = 128
MASKED = -1e30
SCALE2 = HD ** (-0.5) * math.log2(math.e)
VMEM = pl.BlockSpec(memory_space=pltpu.VMEM)
SMEM = pl.BlockSpec(memory_space=pltpu.SMEM)


ANY = pl.BlockSpec(memory_space=pl.ANY)


def normalised(mixed):
    inverse = pl.reciprocal(mixed[:, HD:], approx=True)
    inverse = inverse * (2.0 - mixed[:, HD:] * inverse)
    return (mixed[:, :HD] * inverse).astype(jnp.bfloat16)


class Tiles:
    def __init__(self, shards, span, heads, q_ref, doc_ref, m_ref, acc_ref):
        self.span, self.heads = span, heads
        self.q_ref, self.doc_ref, self.m_ref, self.acc_ref = q_ref, doc_ref, m_ref, acc_ref
        self.me = lax.axis_index("ctx")
        self.per_span = span // BLK
        self.chunk = min(span, 2 * BLK)
        self.blocks = self.chunk // BLK
        self.chunks = span // self.chunk
        self.spans = (self.me, 2 * shards - 1 - self.me)
        row_in = lax.broadcasted_iota(jnp.int32, (BLK, BLK), 0)
        col_in = lax.broadcasted_iota(jnp.int32, (BLK, BLK), 1)
        self.triangle = jnp.where(col_in <= row_in, 0.0, MASKED).astype(jnp.float32)

    def query_block(self, t, query_chunk):
        return self.spans[t] * self.per_span + query_chunk * self.blocks

    def tile(self, t, query_chunk, source, key_block, key_blocks, diagonal=False, o_ref=None, send=None):
        keys, key_row, values, value_row = source
        key_rows = pl.ds(pl.multiple_of(key_row, BLK), key_blocks * BLK)
        value_rows = pl.ds(pl.multiple_of(value_row, BLK), key_blocks * BLK)
        rows = pl.ds(pl.multiple_of(t * self.span + query_chunk * self.chunk, BLK), self.chunk)
        query_block = self.query_block(t, query_chunk)
        bias = {}
        for a in range(self.blocks):
            for c in range(key_blocks):
                same = self.doc_ref[query_block + a] == self.doc_ref[key_block + c]
                if diagonal and c > a:
                    same = jnp.bool_(False)
                bias[a, c] = jnp.where(same, 0.0, MASKED).astype(jnp.float32)
        key = keys[key_rows, :]
        ones = jnp.ones((key_blocks * BLK, HD), jnp.bfloat16)
        value = jnp.concatenate([values[value_rows, :], ones], axis=1)
        for h in range(self.heads):
            query = self.q_ref[rows, h * HD : (h + 1) * HD]
            scores = lax.dot_general(
                query, key, (((1,), (1,)), ((), ())), preferred_element_type=jnp.float32
            )
            lines, peaks = [], []
            for a in range(self.blocks):
                line = []
                for c in range(key_blocks):
                    part = scores[a * BLK : (a + 1) * BLK, c * BLK : (c + 1) * BLK]
                    part = part * SCALE2
                    if diagonal and a == c:
                        part = part + self.triangle
                    elif diagonal or (a, c) != (0, key_blocks - 1):
                        part = part + bias[a, c]
                    line.append(part)
                top = line[0]
                for part in line[1:]:
                    top = jnp.maximum(top, part)
                peaks.append(jnp.broadcast_to(jnp.max(top, axis=1, keepdims=True), (BLK, HD)))
                lines.append(line)
            peak = jnp.concatenate(peaks, axis=0)
            if not diagonal:
                before = self.m_ref[h, rows, :]
                peak = jnp.maximum(peak, before)
            weights = jnp.concatenate(
                [
                    jnp.concatenate(
                        [
                            jnp.exp2(part - peak[a * BLK : (a + 1) * BLK])
                            for part in line
                        ],
                        axis=1,
                    )
                    for a, line in enumerate(lines)
                ],
                axis=0,
            ).astype(jnp.bfloat16)
            mixed = jnp.dot(weights, value, preferred_element_type=jnp.float32)
            if not diagonal:
                shrink = jnp.exp2(before - peak)
                mixed = mixed + self.acc_ref[h, rows, :] * jnp.concatenate([shrink, shrink], axis=1)
            if o_ref is None:
                self.m_ref[h, rows, :] = peak
                self.acc_ref[h, rows, :] = mixed
            else:
                o_ref[rows, h * HD : (h + 1) * HD] = normalised(mixed)
                send(t, h).start()

    def reaches(self, t, query_chunk, key_block, key_blocks):
        last = self.doc_ref[key_block + key_blocks - 1]
        return last == self.doc_ref[self.query_block(t, query_chunk)]

    def earlier(self, t, query_chunk, source, key_block, key_blocks, valid=True):
        @pl.when(self.reaches(t, query_chunk, key_block, key_blocks) & valid)
        def _():
            self.tile(t, query_chunk, source, key_block, key_blocks)

    def whole_span(self, t, source, key_span, valid=True):
        keys, key_row, values, value_row = source

        def step(index, carry):
            query_chunk, key_chunk = index // self.chunks, index % self.chunks
            row = key_chunk * self.chunk
            self.earlier(
                t,
                query_chunk,
                (keys, key_row + row, values, value_row + row),
                key_span * self.per_span + key_chunk * self.blocks,
                self.blocks,
                valid,
            )
            return carry

        if self.chunks == 1:
            step(0, 0)
        else:
            lax.fori_loop(0, self.chunks * self.chunks, step, 0)

    def local(self, own, key_row, value_row):
        for t in range(2):

            def step(index, carry, t=t):
                def source(chunk):
                    row = t * self.span + chunk * self.chunk
                    return own, key_row + row, own, value_row + row

                self.tile(
                    t, index, source(index), self.query_block(t, index), self.blocks, diagonal=True
                )

                def before(key_chunk, inner):
                    key_block = self.query_block(t, key_chunk)
                    self.earlier(t, index, source(key_chunk), key_block, self.blocks)
                    return inner

                if self.chunks > 1:
                    lax.fori_loop(0, index, before, 0)
                return carry

            if self.chunks == 1:
                step(0, 0)
            else:
                lax.fori_loop(0, self.chunks, step, 0)
        self.whole_span(1, (own, key_row, own, value_row), self.spans[0])

    def finish(self, t, o_ref):
        rows = pl.ds(t * self.span, self.span)
        for h in range(self.heads):
            o_ref[rows, h * HD : (h + 1) * HD] = normalised(self.acc_ref[h, rows, :])


def gathered_kernel(shards, q_ref, own, doc_ref, all_k, all_v, o_ref, m_ref, acc_ref):
    span, heads = q_ref.shape[0] // 2, q_ref.shape[1] // HD
    tiles = Tiles(shards, span, heads, q_ref, doc_ref, m_ref, acc_ref)
    tiles.local(own, 0, 2 * span)
    for t in range(2):

        def span_step(s, carry, t=t):
            holder = jnp.minimum(s, 2 * shards - 1 - s)
            row = (2 * holder + jnp.where(s < shards, 0, 1)) * span
            other = (s != tiles.spans[0]) if t == 1 else True
            tiles.whole_span(t, (all_k, row, all_v, row), s, other)
            return carry

        lax.fori_loop(0, tiles.spans[t], span_step, 0)
        tiles.finish(t, o_ref)


def partner_span(tiles, shards, r):
    partner = tiles.me ^ r
    return jnp.where(partner < tiles.me, partner, 2 * shards - 1 - partner)


def reads_last(tiles, shards, t):
    key_span = partner_span(tiles, shards, 3)
    reaches = tiles.reaches(t, 0, key_span * tiles.per_span, tiles.blocks)
    return reaches & (key_span < tiles.spans[t])


def local_kernel(shards, q_hbm, own, doc_ref, q_ref, m_ref, acc_ref, sem):
    heads = q_ref.shape[1] // HD
    span = q_ref.shape[0] // 2
    fetch = pltpu.make_async_copy(q_hbm, q_ref, sem)
    fetch.start()
    fetch.wait()
    Tiles(shards, span, heads, q_ref, doc_ref, m_ref, acc_ref).local(own, 0, 2 * span)


def middle_kernel(shards, q_ref, doc_ref, m_in, acc_in, from2, from1, fix1, fix0, *refs):
    m_ref, acc_ref, o_hbm, o_ref, sems = refs
    heads = q_ref.shape[1] // HD
    span = q_ref.shape[0] // 2
    half = span // 2
    finished = []
    before = Tiles(shards, span, heads, q_ref, doc_ref, m_in, acc_in)
    tiles = Tiles(shards, span, heads, q_ref, doc_ref, m_ref, acc_ref)
    me, per_span, blocks = tiles.me, tiles.per_span, tiles.blocks
    for t in range(2):
        sources = []
        for r, ref in ((2, from2), (1, from1)):
            key_span = partner_span(tiles, shards, r)
            source = (ref, 0, ref, span)
            sources.append((source, key_span * per_span, blocks, key_span < tiles.spans[t]))
        if t == 1:
            half_blocks = half // BLK
            block = jnp.where(me == 0, 3, 2) * per_span + per_span - half_blocks
            middle = (me == 1) | (me == 2)
            sources.append(((fix1, 0, fix1, span), 3 * per_span, blocks, middle))
            sources.append(((fix0, 0, fix0, half), block, half_blocks, me < 2))
        reads = [tiles.reaches(t, 0, block, count) & valid for _, block, count, valid in sources]
        more = reads_last(tiles, shards, t)
        changes = more
        for read in reads:
            changes = changes | read

        @pl.when(changes)
        def _(t=t):
            rows = pl.ds(t * span, span)
            m_ref[:, rows, :] = m_in[:, rows, :]
            acc_ref[:, rows, :] = acc_in[:, rows, :]

        for read, (source, block, count, _) in zip(reads, sources):

            @pl.when(read)
            def _(t=t, source=source, block=block, count=count):
                tiles.tile(t, 0, source, block, count)

        @pl.when(changes & jnp.logical_not(more))
        def _(t=t):
            tiles.finish(t, o_ref)

        @pl.when(jnp.logical_not(changes))
        def _(t=t):
            before.finish(t, o_ref)

        rows = pl.ds(t * span, span)
        copy = pltpu.make_async_copy(o_ref.at[rows], o_hbm.at[rows], sems.at[t])
        finished.append((jnp.logical_not(more), copy))

        @pl.when(jnp.logical_not(more))
        def _(copy=copy):
            copy.start()

    for condition, copy in finished:

        @pl.when(condition)
        def _(copy=copy):
            copy.wait()


def last_kernel(shards, q_ref, doc_ref, m_ref, acc_ref, from3, _, o_hbm, o_ref, sems):
    heads = q_ref.shape[1] // HD
    span = q_ref.shape[0] // 2
    tiles = Tiles(shards, span, heads, q_ref, doc_ref, m_ref, acc_ref)
    key_block = partner_span(tiles, shards, 3) * tiles.per_span
    reads = [reads_last(tiles, shards, t) for t in range(2)]

    def send(t, h):
        part = (pl.ds(t * span, span), pl.ds(h * HD, HD))
        return pltpu.make_async_copy(o_ref.at[part], o_hbm.at[part], sems.at[t, h])

    for t in range(2):

        @pl.when(reads[t])
        def _(t=t):
            source = (from3, 0, from3, span)
            tiles.tile(t, 0, source, key_block, tiles.blocks, o_ref=o_ref, send=send)

    for t in range(2):

        @pl.when(reads[t])
        def _(t=t):
            for h in range(heads):
                send(t, h).wait()


def plan_kernel(doc_ref, plan_ref):
    per_span = doc_ref.shape[0] // 8

    def reads(t, s):
        return doc_ref[(s + 1) * per_span - 1] == doc_ref[t * per_span]

    across = jnp.where(reads(6, 2), 3, jnp.where(reads(7, 3), 4, 2))
    plan_ref[0] = jnp.where(reads(6, 3), across, jnp.where(reads(5, 3), 1, 0))


def body(queries, keys, values, doc_blocks):
    shards = lax.axis_size("ctx")
    rows, heads = queries.shape[0], queries.shape[1] // HD
    span = rows // 2
    params = pltpu.CompilerParams(vmem_limit_bytes=16 * 1024 * 1024)
    state_shapes = [
        jax.ShapeDtypeStruct((heads, rows, HD), jnp.float32),
        jax.ShapeDtypeStruct((heads, rows, 2 * HD), jnp.float32),
    ]
    state_scratch = [pltpu.VMEM(x.shape, x.dtype) for x in state_shapes]
    out_shape = jax.ShapeDtypeStruct(queries.shape, jnp.bfloat16)

    if shards != 4:
        received = [lax.all_gather(x, "ctx", axis=0, tiled=True) for x in (keys, values)]
        return pl.pallas_call(
            lambda *refs: gathered_kernel(shards, *refs),
            in_specs=[VMEM, VMEM, SMEM, VMEM, VMEM],
            out_specs=VMEM,
            out_shape=out_shape,
            scratch_shapes=state_scratch,
            compiler_params=params,
            name="attend",
        )(queries, jnp.concatenate([keys, values]), doc_blocks, *received)

    me = lax.axis_index("ctx")

    def swap(array, r):
        return lax.ppermute(array, "ctx", [(i, i ^ r) for i in range(shards)])

    def send(array, *pairs):
        return lax.ppermute(array, "ctx", pairs)

    own = lax.optimization_barrier(jnp.concatenate([keys, values], axis=0))

    def span_for(r, own):
        row = jnp.where((me ^ r) > me, 0, span)
        parts = [lax.dynamic_slice_in_dim(own, row + base, span, 0) for base in (0, rows)]
        return jnp.concatenate(parts, axis=0)

    def lower_rows(start):
        return jnp.concatenate([own[start:span], own[rows + start : rows + span]], axis=0)

    far = span_for(2, own)
    far, own = lax.optimization_barrier((far, own))
    near, lower, half = span_for(1, own), lower_rows(0), lower_rows(span // 2)
    from2, from1, from3 = swap(far, 2), swap(near, 1), swap(far, 3)
    plan = pl.pallas_call(
        plan_kernel,
        in_specs=[SMEM],
        out_specs=SMEM,
        out_shape=jax.ShapeDtypeStruct((1,), jnp.int32),
        name="plan",
    )(doc_blocks)

    def narrow(lower, half):
        return lower, half

    def beside(lower, half):
        return send(lower, (3, 2)), half

    def across(lower, half):
        return send(lower, (3, 1)) + send(lower, (3, 2)), half

    def across_from_2(lower, half):
        fix1 = send(lower, (3, 1))
        fix0 = send(half, (2, 1))
        return fix1 + send(lower, (3, 2)), fix0

    def across_to_7(lower, half):
        fix1, fix0 = send(half, (3, 1)), send(half, (3, 0))
        second = fix1 + send(half, (3, 2))
        blank = jnp.zeros_like(second[: span // 2])
        parts = [blank, second[: span // 2], blank, second[span // 2 :]]
        return jnp.concatenate(parts, axis=0), fix0

    branches = [narrow, beside, across, across_from_2, across_to_7]
    fixes = lax.switch(plan[0], branches, lower, half)
    q, m, acc = pl.pallas_call(
        lambda *refs: local_kernel(shards, *refs),
        in_specs=[ANY, VMEM, SMEM],
        out_specs=[VMEM] * 3,
        out_shape=[out_shape] + state_shapes,
        scratch_shapes=[pltpu.SemaphoreType.DMA],
        compiler_params=params,
        name="local",
    )(queries, own, doc_blocks)
    m, acc, part = pl.pallas_call(
        lambda *refs: middle_kernel(shards, *refs),
        in_specs=[VMEM, SMEM] + [VMEM] * 6,
        out_specs=[VMEM, VMEM, ANY],
        out_shape=state_shapes + [out_shape],
        scratch_shapes=[
            pltpu.VMEM(out_shape.shape, out_shape.dtype),
            pltpu.SemaphoreType.DMA((2,)),
        ],
        compiler_params=params,
        name="middle",
    )(q, doc_blocks, m, acc, from2, from1, *fixes)
    return pl.pallas_call(
        lambda *refs: last_kernel(shards, *refs),
        in_specs=[VMEM, SMEM, VMEM, VMEM, VMEM, ANY],
        out_specs=ANY,
        out_shape=out_shape,
        input_output_aliases={5: 0},
        scratch_shapes=[
            pltpu.VMEM(out_shape.shape, out_shape.dtype),
            pltpu.SemaphoreType.DMA((2, heads)),
        ],
        compiler_params=params,
        name="last",
    )(q, doc_blocks, m, acc, from3, part)


def solution(mesh):
    return jax.shard_map(
        body,
        mesh=mesh,
        in_specs=(P("ctx", "tp"), P("ctx", "tp"), P("ctx", "tp"), P()),
        out_specs=P("ctx", "tp"),
        check_vma=False,
    )
```

```python
import math

import jax
import jax.numpy as jnp
from jax import lax
from jax.experimental import pallas as pl
from jax.experimental.pallas import tpu as pltpu
from jax.sharding import PartitionSpec as P

HD = 128
BLK = 128
MASKED = -1e30
SCALE2 = HD ** (-0.5) * math.log2(math.e)
VMEM = pl.BlockSpec(memory_space=pltpu.VMEM)
SMEM = pl.BlockSpec(memory_space=pltpu.SMEM)


ANY = pl.BlockSpec(memory_space=pl.ANY)


def normalised(mixed):
    inverse = pl.reciprocal(mixed[:, HD:], approx=True)
    inverse = inverse * (2.0 - mixed[:, HD:] * inverse)
    return (mixed[:, :HD] * inverse).astype(jnp.bfloat16)


class Tiles:
    def __init__(self, shards, span, heads, q_ref, doc_ref, m_ref, acc_ref):
        self.span, self.heads = span, heads
        self.q_ref, self.doc_ref, self.m_ref, self.acc_ref = q_ref, doc_ref, m_ref, acc_ref
        self.me = lax.axis_index("ctx")
        self.per_span = span // BLK
        self.chunk = min(span, 2 * BLK)
        self.blocks = self.chunk // BLK
        self.chunks = span // self.chunk
        self.spans = (self.me, 2 * shards - 1 - self.me)
        row_in = lax.broadcasted_iota(jnp.int32, (BLK, BLK), 0)
        col_in = lax.broadcasted_iota(jnp.int32, (BLK, BLK), 1)
        self.triangle = jnp.where(col_in <= row_in, 0.0, MASKED).astype(jnp.float32)

    def query_block(self, t, query_chunk):
        return self.spans[t] * self.per_span + query_chunk * self.blocks

    def tile(self, t, query_chunk, source, key_block, key_blocks, diagonal=False, o_ref=None, send=None):
        keys, key_row, values, value_row = source
        key_rows = pl.ds(pl.multiple_of(key_row, BLK), key_blocks * BLK)
        value_rows = pl.ds(pl.multiple_of(value_row, BLK), key_blocks * BLK)
        rows = pl.ds(pl.multiple_of(t * self.span + query_chunk * self.chunk, BLK), self.chunk)
        query_block = self.query_block(t, query_chunk)
        bias = {}
        for a in range(self.blocks):
            for c in range(key_blocks):
                same = self.doc_ref[query_block + a] == self.doc_ref[key_block + c]
                bias[a, c] = jnp.where(same, 0.0, MASKED).astype(jnp.float32)
        key = keys[key_rows, :]
        ones = jnp.ones((key_blocks * BLK, HD), jnp.bfloat16)
        value = jnp.concatenate([values[value_rows, :], ones], axis=1)
        for h in range(self.heads):
            query = self.q_ref[rows, h * HD : (h + 1) * HD]
            scores = lax.dot_general(
                query, key, (((1,), (1,)), ((), ())), preferred_element_type=jnp.float32
            )
            lines, peaks = [], []
            for a in range(self.blocks):
                line = []
                for c in range(a + 1 if diagonal else key_blocks):
                    part = scores[a * BLK : (a + 1) * BLK, c * BLK : (c + 1) * BLK]
                    part = part * SCALE2
                    if diagonal and a == c:
                        part = part + self.triangle
                    elif diagonal or (a, c) != (0, key_blocks - 1):
                        part = part + bias[a, c]
                    line.append(part)
                top = line[0]
                for part in line[1:]:
                    top = jnp.maximum(top, part)
                peaks.append(jnp.broadcast_to(jnp.max(top, axis=1, keepdims=True), (BLK, HD)))
                lines.append(line)
            peak = jnp.concatenate(peaks, axis=0)
            if not diagonal:
                before = self.m_ref[h, rows, :]
                peak = jnp.maximum(peak, before)
            weights = jnp.concatenate(
                [
                    jnp.concatenate(
                        [
                            jnp.exp2(part - peak[a * BLK : (a + 1) * BLK])
                            for part in line
                        ]
                        + [jnp.zeros((BLK, BLK), jnp.float32)] * (key_blocks - len(line)),
                        axis=1,
                    )
                    for a, line in enumerate(lines)
                ],
                axis=0,
            ).astype(jnp.bfloat16)
            mixed = jnp.dot(weights, value, preferred_element_type=jnp.float32)
            if not diagonal:
                shrink = jnp.exp2(before - peak)
                mixed = mixed + self.acc_ref[h, rows, :] * jnp.concatenate([shrink, shrink], axis=1)
            if o_ref is None:
                self.m_ref[h, rows, :] = peak
                self.acc_ref[h, rows, :] = mixed
            else:
                o_ref[rows, h * HD : (h + 1) * HD] = normalised(mixed)
                send(t, h).start()

    def reaches(self, t, query_chunk, key_block, key_blocks):
        last = self.doc_ref[key_block + key_blocks - 1]
        return last == self.doc_ref[self.query_block(t, query_chunk)]

    def earlier(self, t, query_chunk, source, key_block, key_blocks, valid=True):
        @pl.when(self.reaches(t, query_chunk, key_block, key_blocks) & valid)
        def _():
            self.tile(t, query_chunk, source, key_block, key_blocks)

    def whole_span(self, t, source, key_span, valid=True):
        keys, key_row, values, value_row = source

        def step(index, carry):
            query_chunk, key_chunk = index // self.chunks, index % self.chunks
            row = key_chunk * self.chunk
            self.earlier(
                t,
                query_chunk,
                (keys, key_row + row, values, value_row + row),
                key_span * self.per_span + key_chunk * self.blocks,
                self.blocks,
                valid,
            )
            return carry

        if self.chunks == 1:
            step(0, 0)
        else:
            lax.fori_loop(0, self.chunks * self.chunks, step, 0)

    def local(self, own, key_row, value_row):
        for t in range(2):

            def step(index, carry, t=t):
                def source(chunk):
                    row = t * self.span + chunk * self.chunk
                    return own, key_row + row, own, value_row + row

                self.tile(
                    t, index, source(index), self.query_block(t, index), self.blocks, diagonal=True
                )

                def before(key_chunk, inner):
                    key_block = self.query_block(t, key_chunk)
                    self.earlier(t, index, source(key_chunk), key_block, self.blocks)
                    return inner

                if self.chunks > 1:
                    lax.fori_loop(0, index, before, 0)
                return carry

            if self.chunks == 1:
                step(0, 0)
            else:
                lax.fori_loop(0, self.chunks, step, 0)
        self.whole_span(1, (own, key_row, own, value_row), self.spans[0])

    def finish(self, t, o_ref):
        rows = pl.ds(t * self.span, self.span)
        for h in range(self.heads):
            o_ref[rows, h * HD : (h + 1) * HD] = normalised(self.acc_ref[h, rows, :])


def gathered_kernel(shards, q_ref, own, doc_ref, all_k, all_v, o_ref, m_ref, acc_ref):
    span, heads = q_ref.shape[0] // 2, q_ref.shape[1] // HD
    tiles = Tiles(shards, span, heads, q_ref, doc_ref, m_ref, acc_ref)
    tiles.local(own, 0, 2 * span)
    for t in range(2):

        def span_step(s, carry, t=t):
            holder = jnp.minimum(s, 2 * shards - 1 - s)
            row = (2 * holder + jnp.where(s < shards, 0, 1)) * span
            other = (s != tiles.spans[0]) if t == 1 else True
            tiles.whole_span(t, (all_k, row, all_v, row), s, other)
            return carry

        lax.fori_loop(0, tiles.spans[t], span_step, 0)
        tiles.finish(t, o_ref)


def partner_span(tiles, shards, r):
    partner = tiles.me ^ r
    return jnp.where(partner < tiles.me, partner, 2 * shards - 1 - partner)


def reads_last(tiles, shards, t):
    key_span = partner_span(tiles, shards, 3)
    reaches = tiles.reaches(t, 0, key_span * tiles.per_span, tiles.blocks)
    return reaches & (key_span < tiles.spans[t])


def local_kernel(shards, q_hbm, own, doc_ref, q_ref, m_ref, acc_ref, sem):
    heads = q_ref.shape[1] // HD
    span = q_ref.shape[0] // 2
    fetch = pltpu.make_async_copy(q_hbm, q_ref, sem)
    fetch.start()
    fetch.wait()
    Tiles(shards, span, heads, q_ref, doc_ref, m_ref, acc_ref).local(own, 0, 2 * span)


def middle_kernel(shards, q_ref, doc_ref, m_in, acc_in, from2, from1, fix1, fix0, *refs):
    m_ref, acc_ref, o_hbm, o_ref, sems = refs
    heads = q_ref.shape[1] // HD
    span = q_ref.shape[0] // 2
    half = span // 2
    finished = []
    before = Tiles(shards, span, heads, q_ref, doc_ref, m_in, acc_in)
    tiles = Tiles(shards, span, heads, q_ref, doc_ref, m_ref, acc_ref)
    me, per_span, blocks = tiles.me, tiles.per_span, tiles.blocks
    for t in range(2):
        sources = []
        for r, ref in ((2, from2), (1, from1)):
            key_span = partner_span(tiles, shards, r)
            source = (ref, 0, ref, span)
            sources.append((source, key_span * per_span, blocks, key_span < tiles.spans[t]))
        if t == 1:
            half_blocks = half // BLK
            block = jnp.where(me == 0, 3, 2) * per_span + per_span - half_blocks
            middle = (me == 1) | (me == 2)
            sources.append(((fix1, 0, fix1, span), 3 * per_span, blocks, middle))
            sources.append(((fix0, 0, fix0, half), block, half_blocks, me < 2))
        reads = [tiles.reaches(t, 0, block, count) & valid for _, block, count, valid in sources]
        more = reads_last(tiles, shards, t)
        changes = more
        for read in reads:
            changes = changes | read

        @pl.when(changes)
        def _(t=t):
            rows = pl.ds(t * span, span)
            m_ref[:, rows, :] = m_in[:, rows, :]
            acc_ref[:, rows, :] = acc_in[:, rows, :]

        for read, (source, block, count, _) in zip(reads, sources):

            @pl.when(read)
            def _(t=t, source=source, block=block, count=count):
                tiles.tile(t, 0, source, block, count)

        @pl.when(changes & jnp.logical_not(more))
        def _(t=t):
            tiles.finish(t, o_ref)

        @pl.when(jnp.logical_not(changes))
        def _(t=t):
            before.finish(t, o_ref)

        rows = pl.ds(t * span, span)
        copy = pltpu.make_async_copy(o_ref.at[rows], o_hbm.at[rows], sems.at[t])
        finished.append((jnp.logical_not(more), copy))

        @pl.when(jnp.logical_not(more))
        def _(copy=copy):
            copy.start()

    for condition, copy in finished:

        @pl.when(condition)
        def _(copy=copy):
            copy.wait()


def last_kernel(shards, q_ref, doc_ref, m_ref, acc_ref, from3, _, o_hbm, o_ref, sems):
    heads = q_ref.shape[1] // HD
    span = q_ref.shape[0] // 2
    tiles = Tiles(shards, span, heads, q_ref, doc_ref, m_ref, acc_ref)
    key_block = partner_span(tiles, shards, 3) * tiles.per_span
    reads = [reads_last(tiles, shards, t) for t in range(2)]

    def send(t, h):
        part = (pl.ds(t * span, span), pl.ds(h * HD, HD))
        return pltpu.make_async_copy(o_ref.at[part], o_hbm.at[part], sems.at[t, h])

    for t in range(2):

        @pl.when(reads[t])
        def _(t=t):
            source = (from3, 0, from3, span)
            tiles.tile(t, 0, source, key_block, tiles.blocks, o_ref=o_ref, send=send)

    for t in range(2):

        @pl.when(reads[t])
        def _(t=t):
            for h in range(heads):
                send(t, h).wait()


def plan_kernel(doc_ref, plan_ref):
    per_span = doc_ref.shape[0] // 8

    def reads(t, s):
        return doc_ref[(s + 1) * per_span - 1] == doc_ref[t * per_span]

    across = jnp.where(reads(6, 2), 3, jnp.where(reads(7, 3), 4, 2))
    plan_ref[0] = jnp.where(reads(6, 3), across, jnp.where(reads(5, 3), 1, 0))


def body(queries, keys, values, doc_blocks):
    shards = lax.axis_size("ctx")
    rows, heads = queries.shape[0], queries.shape[1] // HD
    span = rows // 2
    params = pltpu.CompilerParams(vmem_limit_bytes=16 * 1024 * 1024)
    state_shapes = [
        jax.ShapeDtypeStruct((heads, rows, HD), jnp.float32),
        jax.ShapeDtypeStruct((heads, rows, 2 * HD), jnp.float32),
    ]
    state_scratch = [pltpu.VMEM(x.shape, x.dtype) for x in state_shapes]
    out_shape = jax.ShapeDtypeStruct(queries.shape, jnp.bfloat16)

    if shards != 4:
        received = [lax.all_gather(x, "ctx", axis=0, tiled=True) for x in (keys, values)]
        return pl.pallas_call(
            lambda *refs: gathered_kernel(shards, *refs),
            in_specs=[VMEM, VMEM, SMEM, VMEM, VMEM],
            out_specs=VMEM,
            out_shape=out_shape,
            scratch_shapes=state_scratch,
            compiler_params=params,
            name="attend",
        )(queries, jnp.concatenate([keys, values]), doc_blocks, *received)

    me = lax.axis_index("ctx")

    def swap(array, r):
        return lax.ppermute(array, "ctx", [(i, i ^ r) for i in range(shards)])

    def send(array, *pairs):
        return lax.ppermute(array, "ctx", pairs)

    own = lax.optimization_barrier(jnp.concatenate([keys, values], axis=0))

    def span_for(r, own):
        row = jnp.where((me ^ r) > me, 0, span)
        parts = [lax.dynamic_slice_in_dim(own, row + base, span, 0) for base in (0, rows)]
        return jnp.concatenate(parts, axis=0)

    def lower_rows(start):
        return jnp.concatenate([own[start:span], own[rows + start : rows + span]], axis=0)

    far = span_for(2, own)
    far, own = lax.optimization_barrier((far, own))
    near, lower, half = span_for(1, own), lower_rows(0), lower_rows(span // 2)
    from2, from1, from3 = swap(far, 2), swap(near, 1), swap(far, 3)
    plan = pl.pallas_call(
        plan_kernel,
        in_specs=[SMEM],
        out_specs=SMEM,
        out_shape=jax.ShapeDtypeStruct((1,), jnp.int32),
        name="plan",
    )(doc_blocks)

    def narrow(lower, half):
        return lower, half

    def beside(lower, half):
        return send(lower, (3, 2)), half

    def across(lower, half):
        return send(lower, (3, 1)) + send(lower, (3, 2)), half

    def across_from_2(lower, half):
        fix1 = send(lower, (3, 1))
        fix0 = send(half, (2, 1))
        return fix1 + send(lower, (3, 2)), fix0

    def across_to_7(lower, half):
        fix1, fix0 = send(half, (3, 1)), send(half, (3, 0))
        second = fix1 + send(half, (3, 2))
        blank = jnp.zeros_like(second[: span // 2])
        parts = [blank, second[: span // 2], blank, second[span // 2 :]]
        return jnp.concatenate(parts, axis=0), fix0

    branches = [narrow, beside, across, across_from_2, across_to_7]
    fixes = lax.switch(plan[0], branches, lower, half)
    q, m, acc = pl.pallas_call(
        lambda *refs: local_kernel(shards, *refs),
        in_specs=[ANY, VMEM, SMEM],
        out_specs=[VMEM] * 3,
        out_shape=[out_shape] + state_shapes,
        scratch_shapes=[pltpu.SemaphoreType.DMA],
        compiler_params=params,
        name="local",
    )(queries, own, doc_blocks)
    m, acc, part = pl.pallas_call(
        lambda *refs: middle_kernel(shards, *refs),
        in_specs=[VMEM, SMEM] + [VMEM] * 6,
        out_specs=[VMEM, VMEM, ANY],
        out_shape=state_shapes + [out_shape],
        scratch_shapes=[
            pltpu.VMEM(out_shape.shape, out_shape.dtype),
            pltpu.SemaphoreType.DMA((2,)),
        ],
        compiler_params=params,
        name="middle",
    )(q, doc_blocks, m, acc, from2, from1, *fixes)
    return pl.pallas_call(
        lambda *refs: last_kernel(shards, *refs),
        in_specs=[VMEM, SMEM, VMEM, VMEM, VMEM, ANY],
        out_specs=ANY,
        out_shape=out_shape,
        input_output_aliases={5: 0},
        scratch_shapes=[
            pltpu.VMEM(out_shape.shape, out_shape.dtype),
            pltpu.SemaphoreType.DMA((2, heads)),
        ],
        compiler_params=params,
        name="last",
    )(q, doc_blocks, m, acc, from3, part)


def solution(mesh):
    return jax.shard_map(
        body,
        mesh=mesh,
        in_specs=(P("ctx", "tp"), P("ctx", "tp"), P("ctx", "tp"), P()),
        out_specs=P("ctx", "tp"),
        check_vma=False,
    )
```
